256 devices in a mesh: occ: 8 (over y, x_lo), vir: 32 (over z, x_hi, core).
Axes of the slice: x: 4 (x_hi: 2, x_lo: 2; x = x_hi * 2 + x_lo), y: 4, z: 8, core: 2. Of those that a mesh axis runs over, the one named last changes fastest.
Arguments:
- amplitudes: bfloat16 [2048, 800, 800], P('occ', 'vir'), may hold values from -0.0078125 to 0.0078125
- chol_a: bfloat16 [32, 800, 1600], P(None, 'vir', 'occ'), may hold values from -1 to 1
- chol_b: bfloat16 [4, 800, 1600], P(None, 'vir', 'occ'), may hold values from -1 to 1
Outputs:
- residual: float32 [2048, 128], P('occ', 'vir')
The draws below stay inside these ranges and needn't reach their ends.
All inputs are finite; a program needn't handle non-finite values.
Results may differ from the reference program's by a relative error of at most 0.0029.
Values may be sent and summed in bfloat16 or wider, within the bound.
No kernel may reach another device: no remote copies, remote signals or barrier semaphores. Data moves between devices by JAX's collectives and lax.ppermute only.
A program may use at most 128 MiB of HBM per device.

```python
import jax
import jax.numpy as jnp
from jax import lax

NV = 800
NCHOL = 1600
AT = 32
BT = 4
PAIRS = 2048
N_VIR = 32


def block_scale(stream_key, dims, pieces, low, high):
    def one(position, shards_of):
        heights = jax.random.uniform(jax.random.fold_in(jax.random.fold_in(stream_key, 6), position), (shards_of,), jnp.float32, low / len(pieces), high / len(pieces))
        return jnp.repeat(jnp.exp(heights), dims[position] // shards_of).reshape((-1,) + (1,) * (len(dims) - position - 1))

    gain = one(*pieces[0])
    for cut in pieces[1:]:
        gain = gain * one(*cut)
    return gain


def centred(own_key, dims, scale, bound, split=(), dtype=jnp.bfloat16):
    drawn = jax.random.normal(own_key, dims, jnp.float32) * scale
    if len(split) > 0:
        drawn = block_scale(own_key, dims, split, -0.22, 0.18) * drawn
    return jnp.clip(drawn, min=-bound, max=bound).astype(dtype)


def setup_inputs(seed: int = 0) -> dict:
    splits = jax.random.split(jax.random.key(seed), 4)
    return {
        "amplitudes": centred(splits[0], (PAIRS, NV, NV), (NV * NV) ** -0.5, 0.0078125, ((0, 8), (1, 32))),
        "chol_a": centred(splits[1], (AT, NV, NCHOL), 0.158, 1.0, ((1, 32), (2, 8))),
        "chol_b": centred(splits[2], (BT, NV, NCHOL), 0.158, 1.0, ((1, 32), (2, 8))),
    }


def reference(amplitudes, chol_a, chol_b):
    block_c = NV // N_VIR
    tile_cols = AT * BT
    factor_b = chol_b.astype(jnp.float32)

    def one_block(total, start):
        piece_a = lax.dynamic_slice_in_dim(chol_a, start, block_c, 1).astype(jnp.float32)
        integrals = jnp.einsum('acp,bdp->cdab', piece_a, factor_b).astype(jnp.bfloat16)
        amps = lax.dynamic_slice_in_dim(amplitudes, start, block_c, 1).reshape(PAIRS, block_c * NV)
        term = jnp.dot(amps, integrals.reshape(block_c * NV, tile_cols), preferred_element_type=jnp.float32)
        return total + term, None

    starts = (jnp.arange(N_VIR) * block_c).astype(jnp.int32)
    total, unused = lax.scan(one_block, jnp.zeros((PAIRS, tile_cols), jnp.float32), starts)
    return total
```

```python
import jax
import jax.numpy as jnp
from jax import lax
from jax.experimental import pallas as pl
from jax.experimental.pallas import tpu as pltpu
from jax.sharding import Mesh, PartitionSpec as P

AXES = ("y", "xl", "z", "xh", "c")
SIZES = (4, 2, 8, 2, 2)
NZ = SIZES[2]
PAD = 128
LIMIT = 24 * 1024 * 1024


def spread(t, zd, step=5):
    nc, nv, pairs = t.shape

    def kernel(t_ref, out_ref):
        for z in range(NZ):
            out_ref[z, :, :zd] = t_ref[:, z * zd : (z + 1) * zd]
            out_ref[z, :, zd:] = jnp.zeros((step, PAD - zd, pairs), t.dtype)

    return pl.pallas_call(
        kernel,
        grid=(nc // step,),
        in_specs=[pl.BlockSpec((step, nv, pairs), lambda c: (c, 0, 0))],
        out_specs=pl.BlockSpec((NZ, step, PAD, pairs), lambda c: (0, c, 0, 0)),
        out_shape=jax.ShapeDtypeStruct((2 * NZ, nc, PAD, pairs), t.dtype),
        compiler_params=pltpu.CompilerParams(vmem_limit_bytes=LIMIT),
        cost_estimate=pl.CostEstimate(flops=0, bytes_accessed=30_000_000, transcendentals=0),
    )(t).reshape(2 * NZ, nc * PAD, pairs)


def contract(zs, a, bs, t, acc):
    n = len(zs)
    _, cols, pairs = t.shape
    nc = cols // PAD
    na = a.shape[0] // nc
    nd = bs[0].shape[0] // 2

    def kernel(z_ref, a_ref, *refs):
        b_far, (t_far, acc_ref, out_ref, lhs, b_buf, t_buf, sems) = refs[: 2 * n], refs[2 * n :]

        def copies(k):
            slot = k % 2
            pieces = [(b_far[2 * k + half], b_buf.at[slot, half]) for half in range(2)]
            pieces.append((t_far.at[z_ref[k]], t_buf.at[slot]))
            return [
                pltpu.make_async_copy(src, dst, sems.at[slot, i])
                for i, (src, dst) in enumerate(pieces)
            ]

        for copy in copies(0):
            copy.start()
        lhs[...] = jnp.zeros_like(lhs)
        out_ref[...] = acc_ref[...]
        for k in range(n):
            if k + 1 < n:
                for copy in copies(k + 1):
                    copy.start()
            mine = copies(k)
            for half in range(2):
                mine[half].wait()
            for half in range(2):
                prod = lax.dot_general(
                    a_ref[...], b_buf[k % 2, half], (((1,), (1,)), ((), ())),
                    preferred_element_type=jnp.float32,
                ).astype(jnp.bfloat16)
                for j in range(2):
                    row = (2 * half + j) * na
                    for c in range(nc):
                        lhs[row : row + na, c * PAD : c * PAD + nd] = prod[
                            c * na : (c + 1) * na, j * nd : (j + 1) * nd
                        ]
            mine[2].wait()
            out_ref[...] += jnp.dot(lhs[...], t_buf[k % 2], preferred_element_type=jnp.float32)

    near, far = pl.BlockSpec(memory_space=pltpu.VMEM), pl.BlockSpec(memory_space=pl.ANY)
    return pl.pallas_call(
        kernel,
        grid_spec=pltpu.PrefetchScalarGridSpec(
            num_scalar_prefetch=1,
            grid=(1,),
            in_specs=[near] + [far] * (1 + len(bs)) + [near],
            out_specs=near,
            scratch_shapes=[
                pltpu.VMEM((acc.shape[0], cols), jnp.bfloat16),
                pltpu.VMEM((2, 2) + bs[0].shape, jnp.bfloat16),
                pltpu.VMEM((2,) + t.shape[1:], jnp.bfloat16),
                pltpu.SemaphoreType.DMA((2, 3)),
            ],
        ),
        out_shape=jax.ShapeDtypeStruct(acc.shape, jnp.float32),
        compiler_params=pltpu.CompilerParams(vmem_limit_bytes=40 * 1024 * 1024),
        cost_estimate=pl.CostEstimate(
            flops=n * 2 * 128 * cols * 1600, bytes_accessed=n * 8_000_000, transcendentals=0
        ),
    )(jnp.stack(zs).astype(jnp.int32), a, *bs, t, acc)


def swap(x):
    return lax.ppermute(x, "c", [(0, 1), (1, 0)])


def after(x, *others):
    return lax.optimization_barrier((x,) + others)[0]


def per_device(amplitudes, chol_a, chol_b):
    pairs, nc, nv = amplitudes.shape
    na, _, npl = chol_a.shape
    nb, nd, _ = chol_b.shape
    core, z = lax.axis_index("c"), lax.axis_index("z")
    zd = nv // NZ

    halves = chol_b.reshape(2, nb // 2, nd, npl)
    mine = lax.dynamic_index_in_dim(halves, core, 0, keepdims=False)
    got = swap(lax.dynamic_index_in_dim(halves, 1 - core, 0, keepdims=False))
    both = jnp.where(core == 0, jnp.stack([mine, got]), jnp.stack([got, mine]))
    send = jnp.broadcast_to(both[None], (16,) + both.shape)
    plane = lax.all_to_all(send, ("y", "xl", "xh"), 0, 0)

    amps = spread(amplitudes.transpose(1, 2, 0), zd)
    a_in = chol_a.transpose(1, 0, 2).reshape(nc * na, npl)
    a_send = jnp.broadcast_to(a_in[None], (8,) + a_in.shape)
    plane, amps, a_send = lax.optimization_barrier((plane, amps, a_send))
    plane = plane.reshape(8, 2, 2, nb // 2, nd, npl)
    own = plane.transpose(3, 1, 2, 4, 0, 5).reshape(nb // 2 * zd, 8 * npl)

    away = [(i * 2 + k, (i + 1 - 2 * k) % NZ * 2 + k) for i in range(NZ) for k in range(2)]
    hop = lambda x: lax.ppermute(x, ("z", "c"), away)
    side = 1 - 2 * core
    m1 = hop(own)
    o0 = swap(own)
    o1 = hop(o0)
    a_all = lax.all_to_all(a_send, ("y", "xl"), 0, 0)
    m2, o2 = hop(m1), hop(o1)
    m3, o3 = hop(m2), hop(o2)
    a = a_all.transpose(1, 0, 2).reshape(nc * na, 8 * npl)

    acc = jnp.zeros((nb * na, pairs), jnp.float32)
    at = lambda k: (z - k * side) % NZ
    m3, a = lax.optimization_barrier((m3, a))
    m4 = hop(m3)
    acc = contract(
        [z, at(1), at(-1), at(2), at(-2)], a,
        [own, o0, m1, o1, swap(o1), swap(m1), m2, o2, swap(o2), swap(m2)], amps, acc,
    )
    m4 = after(m4, acc)
    s4 = swap(m4)
    acc = contract([at(3), at(-3)], a, [m3, o3, swap(o3), swap(m3)], amps, acc)
    acc = contract([at(4)], a, [m4, s4], amps, acc)

    res = acc.reshape(2, nb // 2, na, pairs)
    res = jnp.where(core == 0, res, res[::-1]).reshape(nb, na, pairs).transpose(1, 0, 2)
    parts = lax.all_to_all(res, ("z", "xh", "c"), 0, 0)
    return parts.sum(0).T


def solution(mesh):
    fine = Mesh(mesh.devices.reshape(SIZES), AXES)
    occ, vir = ("y", "xl"), ("z", "xh", "c")
    in_specs = (P(occ, vir, None), P(None, vir, occ), P(None, vir, occ))
    return jax.shard_map(
        per_device, mesh=fine, in_specs=in_specs, out_specs=P(occ, vir), check_vma=False
    )
```

```python
import jax
import jax.numpy as jnp
from jax import lax
from jax.experimental import pallas as pl
from jax.experimental.pallas import tpu as pltpu
from jax.sharding import Mesh, PartitionSpec as P

AXES = ("y", "xl", "z", "xh", "c")
SIZES = (4, 2, 8, 2, 2)
NZ = SIZES[2]
PAD = 128
LIMIT = 24 * 1024 * 1024


def spread(t, zd, step=5):
    nc, nv, pairs = t.shape

    def kernel(t_ref, out_ref):
        for z in range(NZ):
            out_ref[z, :, :zd] = t_ref[:, z * zd : (z + 1) * zd]
            out_ref[z, :, zd:] = jnp.zeros((step, PAD - zd, pairs), t.dtype)

    return pl.pallas_call(
        kernel,
        grid=(nc // step,),
        in_specs=[pl.BlockSpec((step, nv, pairs), lambda c: (c, 0, 0))],
        out_specs=pl.BlockSpec((NZ, step, PAD, pairs), lambda c: (0, c, 0, 0)),
        out_shape=jax.ShapeDtypeStruct((NZ, nc, PAD, pairs), t.dtype),
        compiler_params=pltpu.CompilerParams(vmem_limit_bytes=LIMIT),
        cost_estimate=pl.CostEstimate(flops=0, bytes_accessed=30_000_000, transcendentals=0),
    )(t).reshape(NZ, nc * PAD, pairs)


def contract(zs, a, bs, t, acc):
    n = len(zs)
    _, cols, pairs = t.shape
    nc = cols // PAD
    na = a.shape[0] // nc
    nd = bs[0].shape[0] // 2

    def kernel(z_ref, a_ref, *refs):
        b_far, (t_far, acc_ref, out_ref, lhs, b_buf, t_buf, sems) = refs[: 2 * n], refs[2 * n :]

        def copies(k):
            slot = k % 2
            pieces = [(b_far[2 * k + half], b_buf.at[slot, half]) for half in range(2)]
            pieces.append((t_far.at[z_ref[k]], t_buf.at[slot]))
            return [
                pltpu.make_async_copy(src, dst, sems.at[slot, i])
                for i, (src, dst) in enumerate(pieces)
            ]

        for copy in copies(0):
            copy.start()
        lhs[...] = jnp.zeros_like(lhs)
        out_ref[...] = acc_ref[...]
        for k in range(n):
            mine = copies(k)
            for half in range(2):
                mine[half].wait()
            if k + 1 < n:
                for copy in copies(k + 1):
                    copy.start()
            for half in range(2):
                prod = lax.dot_general(
                    a_ref[...], b_buf[k % 2, half], (((1,), (1,)), ((), ())),
                    preferred_element_type=jnp.float32,
                ).astype(jnp.bfloat16)
                for j in range(2):
                    row = (2 * half + j) * na
                    for c in range(nc):
                        lhs[row : row + na, c * PAD : c * PAD + nd] = prod[
                            c * na : (c + 1) * na, j * nd : (j + 1) * nd
                        ]
            mine[2].wait()
            out_ref[...] += jnp.dot(lhs[...], t_buf[k % 2], preferred_element_type=jnp.float32)

    t, *bs = (pltpu.with_memory_space_constraint(x, pltpu.HBM) for x in (t, *bs))
    a = pltpu.with_memory_space_constraint(a, pltpu.VMEM)
    near, far = pl.BlockSpec(memory_space=pltpu.VMEM), pl.BlockSpec(memory_space=pl.ANY)
    return pl.pallas_call(
        kernel,
        grid_spec=pltpu.PrefetchScalarGridSpec(
            num_scalar_prefetch=1,
            grid=(1,),
            in_specs=[near] + [far] * (1 + len(bs)) + [near],
            out_specs=near,
            scratch_shapes=[
                pltpu.VMEM((acc.shape[0], cols), jnp.bfloat16),
                pltpu.VMEM((2, 2) + bs[0].shape, jnp.bfloat16),
                pltpu.VMEM((2,) + t.shape[1:], jnp.bfloat16),
                pltpu.SemaphoreType.DMA((2, 3)),
            ],
        ),
        out_shape=jax.ShapeDtypeStruct(acc.shape, jnp.float32),
        compiler_params=pltpu.CompilerParams(vmem_limit_bytes=40 * 1024 * 1024),
        cost_estimate=pl.CostEstimate(
            flops=n * 2 * 128 * cols * 1600, bytes_accessed=n * 8_000_000, transcendentals=0
        ),
    )(jnp.stack(zs).astype(jnp.int32), a, *bs, t, acc)


def swap(x):
    return lax.ppermute(x, "c", [(0, 1), (1, 0)])


def after(x, *others):
    return lax.optimization_barrier((x,) + others)[0]


def per_device(amplitudes, chol_a, chol_b):
    pairs, nc, nv = amplitudes.shape
    na, _, npl = chol_a.shape
    nb, nd, _ = chol_b.shape
    core, z = lax.axis_index("c"), lax.axis_index("z")
    zd = nv // NZ

    halves = chol_b.reshape(2, nb // 2, nd, npl)
    send = jnp.broadcast_to(halves[None], (16,) + halves.shape)
    send = send.reshape((32,) + halves.shape[1:])
    plane = lax.all_to_all(send, ("y", "xl", "xh", "c"), 0, 0)

    amps = spread(amplitudes.transpose(1, 2, 0), zd)
    a_in = chol_a.transpose(1, 0, 2).reshape(nc * na, npl)
    a_send = jnp.broadcast_to(a_in[None], (8,) + a_in.shape)
    plane, amps, a_send = lax.optimization_barrier((plane, amps, a_send))
    plane = plane.reshape(8, 2, 2, nb // 2, nd, npl)
    own = plane.transpose(3, 1, 2, 4, 0, 5).reshape(nb // 2 * zd, 8 * npl)

    away = [(i * 2 + k, (i + 1 - 2 * k) % NZ * 2 + k) for i in range(NZ) for k in range(2)]
    hop = lambda x: lax.ppermute(x, ("z", "c"), away)
    side = 1 - 2 * core
    m1 = hop(own)
    o0 = swap(own)
    o1 = hop(o0)
    a_all = lax.all_to_all(a_send, ("y", "xl"), 0, 0)
    m2, o2 = hop(m1), hop(o1)
    m3, o3 = hop(m2), hop(o2)
    a = a_all.transpose(1, 0, 2).reshape(nc * na, 8 * npl)

    acc = jnp.zeros((nb * na, pairs), jnp.float32)
    at = lambda k: (z - k * side) % NZ
    m3, a = lax.optimization_barrier((m3, a))
    m4 = hop(m3)
    acc = contract(
        [z, at(1), at(-1), at(2), at(-2)], a,
        [own, o0, m1, o1, swap(o1), swap(m1), m2, o2, swap(o2), swap(m2)], amps, acc,
    )
    m4 = after(m4, acc)
    s4 = swap(m4)
    acc = contract([at(3), at(-3)], a, [m3, o3, swap(o3), swap(m3)], amps, acc)
    acc = contract([at(4)], a, [m4, s4], amps, acc)

    res = acc.reshape(2, nb // 2, na, pairs)
    res = jnp.where(core == 0, res, res[::-1]).reshape(nb, na, pairs).transpose(1, 0, 2)
    parts = lax.all_to_all(res, ("z", "xh", "c"), 0, 0)
    return parts.sum(0).T


def solution(mesh):
    fine = Mesh(mesh.devices.reshape(SIZES), AXES)
    occ, vir = ("y", "xl"), ("z", "xh", "c")
    in_specs = (P(occ, vir, None), P(None, vir, occ), P(None, vir, occ))
    return jax.shard_map(
        per_device, mesh=fine, in_specs=in_specs, out_specs=P(occ, vir), check_vma=False
    )
```

```python
import jax
import jax.numpy as jnp
from jax import lax
from jax.experimental import pallas as pl
from jax.experimental.pallas import tpu as pltpu
from jax.sharding import Mesh, PartitionSpec as P

AXES = ("y", "xl", "z", "xh", "c")
SIZES = (4, 2, 8, 2, 2)
NZ = SIZES[2]
PAD = 128
LIMIT = 24 * 1024 * 1024


def spread(t, zd, step=5):
    nc, nv, pairs = t.shape

    def kernel(t_ref, out_ref):
        for z in range(NZ):
            out_ref[z, :, :zd] = t_ref[:, z * zd : (z + 1) * zd]
            out_ref[z, :, zd:] = jnp.zeros((step, PAD - zd, pairs), t.dtype)

    return pl.pallas_call(
        kernel,
        grid=(nc // step,),
        in_specs=[pl.BlockSpec((step, nv, pairs), lambda c: (c, 0, 0))],
        out_specs=pl.BlockSpec((NZ, step, PAD, pairs), lambda c: (0, c, 0, 0)),
        out_shape=jax.ShapeDtypeStruct((NZ, nc, PAD, pairs), t.dtype),
        compiler_params=pltpu.CompilerParams(vmem_limit_bytes=LIMIT),
        cost_estimate=pl.CostEstimate(flops=0, bytes_accessed=30_000_000, transcendentals=0),
    )(t).reshape(NZ, nc * PAD, pairs)


def contract(zs, a, bs, t, acc):
    n = len(zs)
    _, cols, pairs = t.shape
    nc = cols // PAD
    na = a.shape[0] // nc
    nd = bs[0].shape[0] // 2

    def kernel(z_ref, a_ref, *refs):
        b_far, (t_far, acc_ref, out_ref, lhs, b_buf, t_buf, sems) = refs[: 2 * n], refs[2 * n :]

        def copies(k):
            slot = k % 2
            pieces = [(b_far[2 * k + half], b_buf.at[slot, half]) for half in range(2)]
            pieces.append((t_far.at[z_ref[k]], t_buf.at[slot]))
            return [
                pltpu.make_async_copy(src, dst, sems.at[slot, i])
                for i, (src, dst) in enumerate(pieces)
            ]

        for copy in copies(0):
            copy.start()
        lhs[...] = jnp.zeros_like(lhs)
        out_ref[...] = acc_ref[...]
        for k in range(n):
            mine = copies(k)
            for half in range(2):
                mine[half].wait()
            if k + 1 < n:
                for copy in copies(k + 1):
                    copy.start()
            for half in range(2):
                prod = lax.dot_general(
                    a_ref[...], b_buf[k % 2, half], (((1,), (1,)), ((), ())),
                    preferred_element_type=jnp.float32,
                ).astype(jnp.bfloat16)
                for j in range(2):
                    row = (2 * half + j) * na
                    for c in range(nc):
                        lhs[row : row + na, c * PAD : c * PAD + nd] = prod[
                            c * na : (c + 1) * na, j * nd : (j + 1) * nd
                        ]
            mine[2].wait()
            out_ref[...] += jnp.dot(lhs[...], t_buf[k % 2], preferred_element_type=jnp.float32)

    t, *bs = (pltpu.with_memory_space_constraint(x, pltpu.HBM) for x in (t, *bs))
    a = pltpu.with_memory_space_constraint(a, pltpu.VMEM)
    near, far = pl.BlockSpec(memory_space=pltpu.VMEM), pl.BlockSpec(memory_space=pl.ANY)
    return pl.pallas_call(
        kernel,
        grid_spec=pltpu.PrefetchScalarGridSpec(
            num_scalar_prefetch=1,
            grid=(1,),
            in_specs=[near] + [far] * (1 + len(bs)) + [near],
            out_specs=near,
            scratch_shapes=[
                pltpu.VMEM((acc.shape[0], cols), jnp.bfloat16),
                pltpu.VMEM((2, 2) + bs[0].shape, jnp.bfloat16),
                pltpu.VMEM((2,) + t.shape[1:], jnp.bfloat16),
                pltpu.SemaphoreType.DMA((2, 3)),
            ],
        ),
        out_shape=jax.ShapeDtypeStruct(acc.shape, jnp.float32),
        compiler_params=pltpu.CompilerParams(vmem_limit_bytes=40 * 1024 * 1024),
        cost_estimate=pl.CostEstimate(
            flops=n * 2 * 128 * cols * 1600, bytes_accessed=n * 8_000_000, transcendentals=0
        ),
    )(jnp.stack(zs).astype(jnp.int32), a, *bs, t, acc)


def swap(x):
    return lax.ppermute(x, "c", [(0, 1), (1, 0)])


def after(x, *others):
    return lax.optimization_barrier((x,) + others)[0]


def per_device(amplitudes, chol_a, chol_b):
    pairs, nc, nv = amplitudes.shape
    na, _, npl = chol_a.shape
    nb, nd, _ = chol_b.shape
    core, z = lax.axis_index("c"), lax.axis_index("z")
    zd = nv // NZ

    halves = chol_b.reshape(2, nb // 2, nd, npl)
    send = jnp.broadcast_to(halves[None], (16,) + halves.shape)
    send = send.reshape((32,) + halves.shape[1:])
    plane = lax.all_to_all(send, ("y", "xl", "xh", "c"), 0, 0)

    a_in = chol_a.transpose(1, 0, 2).reshape(nc * na, npl)
    a_send = jnp.broadcast_to(a_in[None], (8,) + a_in.shape)
    amps = spread(after(amplitudes.transpose(1, 2, 0), a_send), zd)
    plane, amps, a_send = lax.optimization_barrier((plane, amps, a_send))
    plane = plane.reshape(8, 2, 2, nb // 2, nd, npl)
    own = plane.transpose(3, 1, 2, 4, 0, 5).reshape(nb // 2 * zd, 8 * npl)

    away = [(i * 2 + k, (i + 1 - 2 * k) % NZ * 2 + k) for i in range(NZ) for k in range(2)]
    hop = lambda x: lax.ppermute(x, ("z", "c"), away)
    side = 1 - 2 * core
    m1 = hop(own)
    o0 = swap(own)
    o1 = hop(o0)
    a_all = lax.all_to_all(a_send, ("y", "xl"), 0, 0)
    m2, o2 = hop(m1), hop(o1)
    m3, o3 = hop(m2), hop(o2)
    a = a_all.transpose(1, 0, 2).reshape(nc * na, 8 * npl)

    acc = jnp.zeros((nb * na, pairs), jnp.float32)
    at = lambda k: (z - k * side) % NZ
    m3, a = lax.optimization_barrier((m3, a))
    m4 = hop(m3)
    acc = contract(
        [z, at(1), at(-1), at(2), at(-2)], a,
        [own, o0, m1, o1, swap(o1), swap(m1), m2, o2, swap(o2), swap(m2)], amps, acc,
    )
    m4 = after(m4, acc)
    s4 = swap(m4)
    acc = contract([at(3), at(-3)], a, [m3, o3, swap(o3), swap(m3)], amps, acc)
    acc = contract([at(4)], a, [m4, s4], amps, acc)

    res = acc.reshape(2, nb // 2, na, pairs)
    res = jnp.where(core == 0, res, res[::-1]).reshape(nb, na, pairs).transpose(1, 0, 2)
    parts = lax.all_to_all(res, ("z", "xh", "c"), 0, 0)
    return parts.sum(0).T


def solution(mesh):
    fine = Mesh(mesh.devices.reshape(SIZES), AXES)
    occ, vir = ("y", "xl"), ("z", "xh", "c")
    in_specs = (P(occ, vir, None), P(None, vir, occ), P(None, vir, occ))
    return jax.shard_map(
        per_device, mesh=fine, in_specs=in_specs, out_specs=P(occ, vir), check_vma=False
    )
```

```python
import jax
import jax.numpy as jnp
from jax import lax
from jax.experimental import pallas as pl
from jax.experimental.pallas import tpu as pltpu
from jax.sharding import Mesh, PartitionSpec as P

AXES = ("y", "xl", "z", "xh", "c")
SIZES = (4, 2, 8, 2, 2)
NZ = SIZES[2]
PAD = 128
LIMIT = 24 * 1024 * 1024


def spread(t, zd, step=5):
    nc, nv, pairs = t.shape

    def kernel(t_ref, out_ref):
        for z in range(NZ):
            out_ref[z, :, :zd] = t_ref[:, z * zd : (z + 1) * zd]
            out_ref[z, :, zd:] = jnp.zeros((step, PAD - zd, pairs), t.dtype)

    return pl.pallas_call(
        kernel,
        grid=(nc // step,),
        in_specs=[pl.BlockSpec((step, nv, pairs), lambda c: (c, 0, 0))],
        out_specs=pl.BlockSpec((NZ, step, PAD, pairs), lambda c: (0, c, 0, 0)),
        out_shape=jax.ShapeDtypeStruct((NZ, nc, PAD, pairs), t.dtype),
        compiler_params=pltpu.CompilerParams(vmem_limit_bytes=LIMIT),
        cost_estimate=pl.CostEstimate(flops=0, bytes_accessed=30_000_000, transcendentals=0),
    )(t).reshape(NZ, nc * PAD, pairs)


def contract(zs, a, bs, t, acc):
    n = len(zs)
    _, cols, pairs = t.shape
    nc = cols // PAD
    na = a.shape[0] // nc
    nd = bs[0].shape[0] // 2

    def kernel(z_ref, a_ref, *refs):
        b_far, (t_far, acc_ref, out_ref, lhs, b_buf, t_buf, sems) = refs[: 2 * n], refs[2 * n :]

        def copies(k):
            slot = k % 2
            pieces = [(b_far[2 * k + half], b_buf.at[slot, half]) for half in range(2)]
            pieces.append((t_far.at[z_ref[k]], t_buf.at[slot]))
            return [
                pltpu.make_async_copy(src, dst, sems.at[slot, i])
                for i, (src, dst) in enumerate(pieces)
            ]

        for copy in copies(0):
            copy.start()
        lhs[...] = jnp.zeros_like(lhs)
        out_ref[...] = acc_ref[...]
        for k in range(n):
            mine = copies(k)
            for half in range(2):
                mine[half].wait()
            if k + 1 < n:
                for copy in copies(k + 1):
                    copy.start()
            for half in range(2):
                prod = lax.dot_general(
                    a_ref[...], b_buf[k % 2, half], (((1,), (1,)), ((), ())),
                    preferred_element_type=jnp.float32,
                ).astype(jnp.bfloat16)
                for j in range(2):
                    row = (2 * half + j) * na
                    for c in range(nc):
                        lhs[row : row + na, c * PAD : c * PAD + nd] = prod[
                            c * na : (c + 1) * na, j * nd : (j + 1) * nd
                        ]
            mine[2].wait()
            out_ref[...] += jnp.dot(lhs[...], t_buf[k % 2], preferred_element_type=jnp.float32)

    t, *bs = (pltpu.with_memory_space_constraint(x, pltpu.HBM) for x in (t, *bs))
    a = pltpu.with_memory_space_constraint(a, pltpu.VMEM)
    near, far = pl.BlockSpec(memory_space=pltpu.VMEM), pl.BlockSpec(memory_space=pl.ANY)
    return pl.pallas_call(
        kernel,
        grid_spec=pltpu.PrefetchScalarGridSpec(
            num_scalar_prefetch=1,
            grid=(1,),
            in_specs=[near] + [far] * (1 + len(bs)) + [near],
            out_specs=near,
            scratch_shapes=[
                pltpu.VMEM((acc.shape[0], cols), jnp.bfloat16),
                pltpu.VMEM((2, 2) + bs[0].shape, jnp.bfloat16),
                pltpu.VMEM((2,) + t.shape[1:], jnp.bfloat16),
                pltpu.SemaphoreType.DMA((2, 3)),
            ],
        ),
        out_shape=jax.ShapeDtypeStruct(acc.shape, jnp.float32),
        compiler_params=pltpu.CompilerParams(vmem_limit_bytes=24 * 1024 * 1024),
        cost_estimate=pl.CostEstimate(
            flops=n * 2 * 128 * cols * 1600, bytes_accessed=n * 8_000_000, transcendentals=0
        ),
    )(jnp.stack(zs).astype(jnp.int32), a, *bs, t, acc)


def swap(x):
    return lax.ppermute(x, "c", [(0, 1), (1, 0)])


def after(x, *others):
    return lax.optimization_barrier((x,) + others)[0]


def per_device(amplitudes, chol_a, chol_b):
    pairs, nc, nv = amplitudes.shape
    na, _, npl = chol_a.shape
    nb, nd, _ = chol_b.shape
    core, z = lax.axis_index("c"), lax.axis_index("z")
    zd = nv // NZ

    halves = chol_b.reshape(2, nb // 2, nd, npl)
    send = jnp.broadcast_to(halves[None], (16,) + halves.shape)
    send = send.reshape((32,) + halves.shape[1:])
    plane = lax.all_to_all(send, ("y", "xl", "xh", "c"), 0, 0)

    a_in = chol_a.transpose(1, 0, 2).reshape(nc * na, npl)
    a_send = jnp.broadcast_to(a_in[None], (8,) + a_in.shape)
    amps = spread(after(amplitudes.transpose(1, 2, 0), a_send), zd)
    plane, amps, a_send = lax.optimization_barrier((plane, amps, a_send))
    plane = plane.reshape(8, 2, 2, nb // 2, nd, npl)
    own = plane.transpose(3, 1, 2, 4, 0, 5).reshape(nb // 2 * zd, 8 * npl)

    away = [(i * 2 + k, (i + 1 - 2 * k) % NZ * 2 + k) for i in range(NZ) for k in range(2)]
    hop = lambda x: lax.ppermute(x, ("z", "c"), away)
    side = 1 - 2 * core
    m1 = hop(own)
    o0 = swap(own)
    o1 = hop(o0)
    a_all = lax.all_to_all(a_send, ("y", "xl"), 0, 0)
    m2, o2 = hop(m1), hop(o1)
    m3, o3 = hop(m2), hop(o2)
    a = a_all.transpose(1, 0, 2).reshape(nc * na, 8 * npl)

    acc = jnp.zeros((nb * na, pairs), jnp.float32)
    at = lambda k: (z - k * side) % NZ
    m3, a = lax.optimization_barrier((m3, a))
    m4 = hop(m3)
    acc = contract(
        [z, at(1), at(-1), at(2), at(-2)], a,
        [own, o0, m1, o1, swap(o1), swap(m1), m2, o2, swap(o2), swap(m2)], amps, acc,
    )
    m4 = after(m4, acc)
    s4 = swap(m4)
    acc = contract([at(3), at(-3)], a, [m3, o3, swap(o3), swap(m3)], amps, acc)
    acc = contract([at(4)], a, [m4, s4], amps, acc)

    res = acc.reshape(2, nb // 2, na, pairs)
    res = jnp.where(core == 0, res, res[::-1]).reshape(nb, na, pairs).transpose(1, 0, 2)
    parts = lax.all_to_all(res, ("z", "xh", "c"), 0, 0)
    return parts.sum(0).T


def solution(mesh):
    fine = Mesh(mesh.devices.reshape(SIZES), AXES)
    occ, vir = ("y", "xl"), ("z", "xh", "c")
    in_specs = (P(occ, vir, None), P(None, vir, occ), P(None, vir, occ))
    return jax.shard_map(
        per_device, mesh=fine, in_specs=in_specs, out_specs=P(occ, vir), check_vma=False
    )
```
